512 devices in a mesh: grp: 4 (over x), gx: 16 (over y, core), gy: 8 (over z).
Axes of the slice: x: 4, y: 8, z: 8, core: 2. Of those that a mesh axis runs over, the one named last changes fastest.
Arguments:
- source: float32 [256, 128, 512], P('gx', 'gy', 'grp'), may hold values from -13 to 13
- conductance: float32 [256, 128, 512], P('gx', 'gy', 'grp'), may hold values from 0.2 to 5
- storage: float32 [256, 128, 512], P('gx', 'gy', 'grp'), may hold values from 0.05 to 1
- aggregate_ids: int32 [256, 128, 512], P('gx', 'gy', 'grp'), may hold values from 0 to 511, as said below
- coarse_values: float32 [4096, 64, 256], P(('grp', 'gx', 'gy')), as said below
- coarse_columns: int32 [4096, 4], P(('grp', 'gx', 'gy')), may hold values from 0 to 4095, as said below
Outputs:
- solution: float32 [256, 128, 512], P('gx', 'gy', 'grp')
- coarse_error: float32 [262144], P(('grp', 'gx', 'gy'))
The draws below stay inside these ranges and needn't reach their ends.
Inputs may be any that keep to these rules, and one draw needn't show every extreme that they name: `aggregate_ids`: on each device, every id names exactly the 64 cells of one aligned 4 x 4 x 4 box of the device's block, and different boxes have different ids. `coarse_columns`: entry 0 of block row b is b itself; every other entry names a block of a device whose gx and gy indices differ from those of row b's device by at most one. `coarse_values`: in every row of the coarse operator the diagonal entry of the first stored block exceeds the sum of the magnitudes of all other stored entries of that row.
All inputs are finite; a program needn't handle non-finite values.
Results may differ from the reference program's by a relative error of at most 0.0001.
Values sent between devices are 32-bit elements; how exact they have to be, the bound alone decides.
A program may use at most 64 MiB of HBM per device.

```python
import math
import jax
import jax.numpy as jnp
from jax import lax

CX = 16
CY = 16
CZ = 128
NU = 2
CITER = 4
K = 4
NX = 256
NY = 128
NZ = 512
NC_DEV = 512
BDEV = 8
NC = 262144
NB = 4096


TWO_PI = 6.283185307179586


def one_permutation(single_key):
    return jax.random.permutation(single_key, NC_DEV).astype(jnp.int32)


def draw_source(key, part):
    key_list = jax.random.split(key, 3)
    phases = jax.random.uniform(key_list[0], (3,), jnp.float32, 0.0, TWO_PI)
    amplitude = jax.random.uniform(key_list[1], (), jnp.float32, 1.5, 2.5)
    rough = jnp.clip(3.0 * jax.random.normal(key_list[2], (NX, NY, NZ), jnp.float32), -9.0, 9.0)
    pos_x = lax.broadcasted_iota(jnp.int32, (NX, NY, NZ), 0).astype(jnp.float32) / NX
    pos_y = lax.broadcasted_iota(jnp.int32, (NX, NY, NZ), 1).astype(jnp.float32) / NY
    pos_z = lax.broadcasted_iota(jnp.int32, (NX, NY, NZ), 2).astype(jnp.float32) / NZ
    wave = jnp.sin(TWO_PI * pos_x + phases[0]) * jnp.sin(TWO_PI * pos_y + phases[1]) * jnp.sin(TWO_PI * pos_z + phases[2])
    return rough + amplitude * (1.0 + 0.5 * wave)


def draw_aggregate_ids(key, part):
    grid_x = NX // CX
    grid_y = NY // CY
    groups = NZ // CZ
    key_list = jax.random.split(key, grid_x * grid_y * groups)
    perm_table = jax.vmap(one_permutation)(key_list)
    cell_x = lax.broadcasted_iota(jnp.int32, (NX, NY, NZ), 0)
    cell_y = lax.broadcasted_iota(jnp.int32, (NX, NY, NZ), 1)
    cell_z = lax.broadcasted_iota(jnp.int32, (NX, NY, NZ), 2)
    device_ids = (cell_z // CZ * grid_x + cell_x // CX) * grid_y + cell_y // CY
    box_ids = (cell_x % CX // 4 * (CY // 4) + cell_y % CY // 4) * (CZ // 4) + cell_z % CZ // 4
    return perm_table[device_ids, box_ids]


def draw_coarse_columns(key, part):
    grid_x = NX // CX
    grid_y = NY // CY
    groups = NZ // CZ
    row_ids = lax.broadcasted_iota(jnp.int32, (NB, K), 0)
    slot_ids = lax.broadcasted_iota(jnp.int32, (NB, K), 1)
    device_ids = row_ids // BDEV
    home_y = device_ids % grid_y
    home_x = device_ids // grid_y % grid_x
    key_list = jax.random.split(key, 4)
    step_x = jax.random.randint(key_list[0], (NB, K), -1, 2)
    step_y = jax.random.randint(key_list[1], (NB, K), -1, 2)
    member_ids = jax.random.randint(key_list[2], (NB, K), 0, groups)
    within_ids = jax.random.randint(key_list[3], (NB, K), 0, BDEV)
    target_x = jnp.clip(home_x + step_x, 0, grid_x - 1)
    target_y = jnp.clip(home_y + step_y, 0, grid_y - 1)
    columns = ((member_ids * grid_x + target_x) * grid_y + target_y) * BDEV + within_ids
    return jnp.where(slot_ids == 0, row_ids, columns).astype(jnp.int32)


def draw_coarse_values(key, part):
    key_list = jax.random.split(key, 2)
    off_part = jax.random.uniform(key_list[0], (NB, 64, K * 64), jnp.float32, 0.5, 1.0)
    main_part = jax.random.uniform(key_list[1], (NB, 64), jnp.float32, 1.01, 1.1)
    identity = jnp.eye(64, dtype=jnp.float32)
    marker = jnp.concatenate([identity, jnp.zeros((64, (K - 1) * 64), jnp.float32)], axis=1)
    leading = (K * 64 - 1) * main_part
    values = -off_part * (1.0 - marker[None]) + marker[None] * leading[:, :, None]
    return values


def block_scale(rng, shape, pieces, smallest, largest):
    level = 1.0
    for dim, blocks in pieces:
        heights = jax.random.uniform(jax.random.fold_in(jax.random.fold_in(rng, 6), dim), (blocks,), jnp.float32, smallest / len(pieces), largest / len(pieces))
        level = level * jnp.repeat(jnp.exp(heights), shape[dim] // blocks).reshape((-1,) + (1,) * (len(shape) - 1 - dim))
    return level


def setup_inputs(seed: int = 0) -> dict:
    splits = jax.random.split(jax.random.key(seed), 7)
    return {
        "source": draw_source(jax.random.fold_in(splits[6], 71), 0),
        "conductance": jnp.clip(jnp.exp(math.log(5.0) - 3.218876 * jax.random.uniform(splits[1], (NX, NY, NZ), jnp.float32) ** block_scale(splits[1], (NX, NY, NZ), ((0, 16), (1, 8), (2, 4)), -0.2, 0.2)), 0.2, 5.0),
        "storage": jnp.clip(jnp.exp(math.log(1.0) - 2.9957323 * jax.random.uniform(splits[2], (NX, NY, NZ), jnp.float32) ** block_scale(splits[2], (NX, NY, NZ), ((0, 16), (1, 8), (2, 4)), -0.2, 0.2)), 0.05, 1.0),
        "aggregate_ids": draw_aggregate_ids(jax.random.fold_in(splits[6], 71), 0),
        "coarse_values": draw_coarse_values(jax.random.fold_in(splits[6], 71), 0),
        "coarse_columns": draw_coarse_columns(jax.random.fold_in(splits[6], 71), 0),
    }


WEIGHT = 2.0 / 3.0
PAIRS = ((0, 1), (0, -1), (1, 1), (1, -1), (2, 1), (2, -1))


def shifted(padded, dimension, offset):
    window = [slice(1, -1), slice(1, -1), slice(1, -1)]
    window[dimension] = slice(1 + offset, padded.shape[dimension] - 1 + offset)
    return padded[tuple(window)]


def face_terms(conductance):
    padded = jnp.pad(conductance, 1)
    return [0.5 * (conductance + shifted(padded, dimension, offset)) for dimension, offset in PAIRS]


def operate(field, storage, face_list):
    padded = jnp.pad(field, 1)
    summed = storage * field
    for position in range(6):
        dimension, offset = PAIRS[position]
        summed = summed + face_list[position] * (field - shifted(padded, dimension, offset))
    return summed


def coarse_apply(vector, coarse_values, coarse_columns):
    blocks = vector.reshape(-1, 64)[coarse_columns]
    blocks = blocks.reshape(blocks.shape[0], -1)
    return jnp.einsum("bim,bm->bi", coarse_values, blocks, precision=lax.Precision.HIGHEST).reshape(-1)


def reference(source, conductance, storage, aggregate_ids, coarse_values, coarse_columns):
    face_list = face_terms(conductance)
    diagonal = storage
    for position in range(6):
        diagonal = diagonal + face_list[position]
    solution = WEIGHT * source / diagonal
    for sweep_number in range(NU - 1):
        solution = solution + WEIGHT * (source - operate(solution, storage, face_list)) / diagonal
    residual = source - operate(solution, storage, face_list)
    smoothed = residual - WEIGHT * operate(residual / diagonal, storage, face_list)
    cell_x = lax.broadcasted_iota(jnp.int32, source.shape, 0)
    cell_y = lax.broadcasted_iota(jnp.int32, source.shape, 1)
    cell_z = lax.broadcasted_iota(jnp.int32, source.shape, 2)
    device_ids = ((cell_z // CZ) * (NX // CX) + cell_x // CX) * (NY // CY) + cell_y // CY
    global_ids = (device_ids * NC_DEV + aggregate_ids).astype(jnp.int32)
    coarse_rhs = jax.ops.segment_sum(smoothed.reshape(-1), global_ids.reshape(-1), num_segments=NC)
    coarse_diag = jnp.diagonal(coarse_values[:, :, :64], axis1=1, axis2=2).reshape(-1)
    coarse_error = coarse_rhs / coarse_diag
    for sweep_number in range(CITER - 1):
        applied = coarse_apply(coarse_error, coarse_values, coarse_columns)
        coarse_error = coarse_error + (coarse_rhs - applied) / coarse_diag
    lifted = coarse_error[global_ids]
    solution = solution + (lifted - WEIGHT * operate(lifted, storage, face_list) / diagonal)
    for sweep_number in range(NU):
        solution = solution + WEIGHT * (source - operate(solution, storage, face_list)) / diagonal
    return (solution, coarse_error)
```

```python
import jax
import jax.numpy as jnp
from jax import lax
from jax.sharding import PartitionSpec as P
import jax.experimental.pallas as pl
import jax.experimental.pallas.tpu as pltpu


F32 = jnp.float32
BF16 = jnp.bfloat16
WEIGHT = 2.0 / 3.0
KEEP = 1.0 / 3.0
NG, NX, NY = 4, 16, 8
MESH = pl.DeviceIdType.MESH
STEPS = (-1, 1)

COARSE = sorted(
    [(g, x, y) for g in range(4) for x in (0, 1, -1) for y in (0, 1, -1) if (g, x, y) != (0, 0, 0)],
    key=lambda d: -(min(d[0], 4 - d[0]) + abs(d[1]) + abs(d[2])),
)


def slot_of(d):
    return (d[0] * 3 + d[1] % 3) * 3 + d[2] % 3


def device(d):
    g, x, y = lax.axis_index("grp"), lax.axis_index("gx"), lax.axis_index("gy")
    return (lax.rem(g + d[0] + NG, NG), lax.rem(x + d[1] + NX, NX), lax.rem(y + d[2] + NY, NY))


def side(step):
    return 0 if step < 0 else 1


def iota(shape, dim):
    return lax.broadcasted_iota(jnp.int32, shape, dim)


def roll(x, shift, axis):
    return pltpu.roll(x, shift, axis)


def arrive(buffer, sem):
    pltpu.make_async_copy(buffer, buffer, sem).wait()


def kernel(
    src, cond, stor, aggr, cval, ccol,
    out, err,
    vC, vS, vB, vA, vV,
    PY8, PY2, PP, PE, PF,
    RXC, RXS, RXB, RY8, RY2, RXY, RP, RF, RE, RK,
    EC, ES, EB, FX, FY, FZ, G, U0, U1, U2, VV, YZ, Q, QE,
    LAB, W, DG, INV, ROWS, PM, GA, EBUF, TS, RB0, RB1, RB2, FF, RLF, RLX, LP,
    lsem, ssem, rsem, cs, cr,
):
    mg, mx, my = lax.axis_index("grp"), lax.axis_index("gx"), lax.axis_index("gy")

    def send(source, target, n, d):
        pltpu.make_async_remote_copy(
            src_ref=source, dst_ref=target, send_sem=ssem.at[n], recv_sem=rsem.at[n],
            device_id=device(d), device_id_type=MESH,
        ).start()

    barrier = pltpu.get_barrier_semaphore()
    for d in COARSE:
        pl.semaphore_signal(barrier, inc=1, device_id=device(d), device_id_type=MESH)
    loads = [(cond, vC), (stor, vS), (src, vB), (cval, vV)]
    loads = [pltpu.make_async_copy(a, b, lsem.at[n]) for n, (a, b) in enumerate(loads)]
    for n in range(4):
        loads.append(pltpu.make_async_copy(aggr.at[4 * n], vA.at[n], lsem.at[4 + n]))
    for copy in loads:
        copy.start()
    for copy in loads[:3]:
        copy.wait()

    PY8[0, :, 0:3, :] = vC[:, 0:3, :]
    PY8[0, :, 3:5, :] = vS[:, 0:2, :]
    PY8[0, :, 5:7, :] = vB[:, 0:2, :]
    PY8[0, :, 7:8, :] = vS[:, 2:3, :]
    PY2[0, :, 0:1, :] = vC[:, 3:4, :]
    PY2[0, :, 1:2, :] = vB[:, 2:3, :]
    PY8[1, :, 0:3, :] = vC[:, 13:16, :]
    PY8[1, :, 3:5, :] = vS[:, 14:16, :]
    PY8[1, :, 5:7, :] = vB[:, 14:16, :]
    PY8[1, :, 7:8, :] = vS[:, 13:14, :]
    PY2[1, :, 0:1, :] = vC[:, 12:13, :]
    PY2[1, :, 1:2, :] = vB[:, 13:14, :]
    lane16 = iota((16, 128), 1)
    packed = [jnp.zeros((16, 128), F32)] * 3
    for x in range(16):
        mine = lane16 // 8 == x
        packed = [jnp.where(mine, roll(v[x], 8 * x + 4, 1), p) for v, p in zip((vC, vS, vB), packed)]
    pc, ps, pb = packed
    PP[0], PP[1], PP[2] = pc, ps, pb
    edge = jnp.where(lane16 < 40, roll(ps, 24, 1), roll(pb, 40, 1))
    edge = jnp.where(lane16 >= 64, roll(pb, 88, 1), edge)
    edge = jnp.where(lane16 >= 88, roll(ps, 104, 1), edge)
    PE[...] = jnp.where((lane16 < 24) | (lane16 >= 104), pc, edge)
    PF[0, 0:3], PF[0, 3:5], PF[0, 5:7] = pc[0:3], ps[0:2], pb[0:2]
    PF[1, 0:3], PF[1, 3:5], PF[1, 5:7] = pc[13:16], ps[14:16], pb[14:16]
    PF[0, 7:8] = pc[0:1]
    PF[1, 7:8] = pc[0:1]

    pl.semaphore_wait(barrier, len(COARSE))
    for b in STEPS:
        send(PY8.at[side(b)], RY8.at[side(b)], 3, (0, 0, b))
        send(PY2.at[side(b)], RY2.at[side(b)], 4, (0, 0, b))
    for a in STEPS:
        for b in STEPS:
            for c in STEPS:
                send(PE.at[pl.ds(8 * side(c), 8)], RK.at[side(a), side(b), side(c)], 9, (a, b, c))
    for a in STEPS:
        send(PP, RP.at[side(a)], 6, (a, 0, 0))
    for b in STEPS:
        s = side(b)
        send(cond.at[pl.ds(12 * s, 4)], RXC.at[s], 0, (0, b, 0))
        send(stor.at[pl.ds(13 * s, 3)], RXS.at[s], 1, (0, b, 0))
        send(src.at[pl.ds(13 * s, 3)], RXB.at[s], 2, (0, b, 0))
    for a in STEPS:
        for b in STEPS:
            send(PE, RE.at[side(a), side(b)], 8, (a, b, 0))
            send(PF.at[side(b)], RF.at[side(a), side(b)], 7, (a, 0, b))
            send(PY8.at[side(b), pl.ds(13 * side(a), 3)], RXY.at[side(a), side(b)], 5, (0, a, b))

    EC[4:20, 4:20, 0:128] = vC[...]
    ES[4:20, 4:20, 0:128] = vS[...]
    EB[4:20, 4:20, 0:128] = vB[...]
    row, lane = iota((24, 256), 0), iota((24, 256), 1)
    inside = ((row >= 4) | (my > 0)) & ((row < 20) | (my < NY - 1))
    inside &= (lane < 128) | ((lane < 132) & (mg < NG - 1)) | ((lane >= 252) & (mg > 0))
    YZ[...] = inside.astype(jnp.int32)
    for copy in loads[3:]:
        copy.wait()
    for r in range(16):
        LAB[r : r + 1, :] = vA[r // 4, 4 * (r % 4) : 4 * (r % 4) + 1, :]

    def invert(r, inv):
        label = LAB[pl.ds(r, 1), :]
        s8, l8 = iota((8, 128), 0), iota((8, 128), 1)
        mine = (label // 128 == s8 % 4) & (l8 % 4 == 0)
        code = jnp.where(mine, jnp.where(s8 < 4, r, l8 // 4), 0).astype(F32).astype(BF16)
        hot = jnp.where(label % 128 == iota((128, 128), 0), 1.0, 0.0).astype(BF16)
        return inv + lax.dot_general(code, hot, (((1,), (1,)), ((), ())), preferred_element_type=F32)

    inv = lax.fori_loop(0, 16, invert, jnp.zeros((8, 128), F32))
    INV[...] = (inv + 0.5).astype(jnp.int32)

    diag_at = iota((64, 128), 0) == iota((64, 128), 1)
    off_at = iota((64, 256), 0) == iota((64, 256), 1)
    lane1 = iota((1, 128), 1)
    for q in range(4):
        two = []
        for b in (2 * q, 2 * q + 1):
            two.append(jnp.sum(jnp.where(diag_at, vV[b, :, 0:128], 0.0), axis=0, keepdims=True))
            block = jnp.where(off_at, 0.0, vV[b])
            high = block.astype(BF16)
            W[64 * b : 64 * b + 64, :] = high
            W[512 + 64 * b : 576 + 64 * b, :] = (block - high.astype(F32)).astype(BF16)
        DG[q : q + 1, :] = jnp.where(lane1 < 64, two[0], roll(two[1], 64, 1))

    def place(r, c):
        k, b = r // 8, r % 8
        column = ccol[b, k]
        owner, block = column >> 3, column & 7
        dg = (mg - (owner >> 7)) & 3
        dx = lax.rem(mx - ((owner >> 3) & 15) + 3, 3)
        dy = lax.rem(my - (owner & 7) + 3, 3)
        ROWS[r] = ((dg * 3 + dx) * 3 + dy) * 4 + (block >> 1)
        PM[pl.ds(r, 1), :] = jnp.full((1, 128), (block + k) & 1, jnp.int32)
        return c

    lax.fori_loop(0, 32, place, 0)

    arrived = (RXC, RXS, RXB, RY8, RY2, RXY, RP, RF, RE, RK)
    for n, buffer in enumerate(arrived):
        arrive(buffer, rsem.at[n])
    fields = (EC, ES, EB)
    EC[20:24, 4:20, 0:128], EC[0:4, 4:20, 0:128] = RXC[0], RXC[1]
    ES[20:23, 4:20, 0:128], ES[1:4, 4:20, 0:128] = RXS[0], RXS[1]
    EB[20:23, 4:20, 0:128], EB[1:4, 4:20, 0:128] = RXB[0], RXB[1]
    EC[4:20, 20:23, 0:128], EC[4:20, 1:4, 0:128] = RY8[0, :, 0:3], RY8[1, :, 0:3]
    EC[4:20, 23:24, 0:128], EC[4:20, 0:1, 0:128] = RY2[0, :, 0:1], RY2[1, :, 0:1]
    ES[4:20, 20:22, 0:128], ES[4:20, 2:4, 0:128] = RY8[0, :, 3:5], RY8[1, :, 3:5]
    ES[4:20, 22:23, 0:128], ES[4:20, 1:2, 0:128] = RY8[0, :, 7:8], RY8[1, :, 7:8]
    EB[4:20, 20:22, 0:128], EB[4:20, 2:4, 0:128] = RY8[0, :, 5:7], RY8[1, :, 5:7]
    EB[4:20, 22:23, 0:128], EB[4:20, 1:2, 0:128] = RY2[0, :, 1:2], RY2[1, :, 1:2]
    for a in (0, 1):
        x0 = 20 - 19 * a
        EC[x0 : x0 + 3, 20:23, 0:128], EC[x0 : x0 + 3, 1:4, 0:128] = RXY[a, 0, :, 0:3], RXY[a, 1, :, 0:3]
        ES[x0 : x0 + 3, 20:22, 0:128], ES[x0 : x0 + 3, 2:4, 0:128] = RXY[a, 0, :, 3:5], RXY[a, 1, :, 3:5]
        EB[x0 : x0 + 3, 20:22, 0:128], EB[x0 : x0 + 3, 2:4, 0:128] = RXY[a, 0, :, 5:7], RXY[a, 1, :, 5:7]
    low = lane16 % 8 < 4
    low8 = low[0:8]
    for n in range(3):
        Q[n, 4:20] = jnp.where(low, RP[1, n], RP[0, n])
    for b in (0, 1):
        rows = jnp.where(low8, RF[1, b], RF[0, b])
        Q[0, (20, 1)[b] : (23, 4)[b]] = rows[0:3]
        Q[1, (20, 2)[b] : (22, 4)[b]] = rows[3:5]
        Q[2, (20, 2)[b] : (22, 4)[b]] = rows[5:7]
    half, half8 = lane16 < 64, lane16[0:8] < 64
    QE[4:20] = jnp.where(low, jnp.where(half, RE[1, 0], RE[1, 1]), jnp.where(half, RE[0, 0], RE[0, 1]))
    for c in (0, 1):
        rows = jnp.where(
            low8, jnp.where(half8, RK[1, 0, c], RK[1, 1, c]), jnp.where(half8, RK[0, 0, c], RK[0, 1, c])
        )
        QE[(20, 1)[c] : (23, 4)[c]] = rows[(0, 5)[c] : (3, 8)[c]]
    for n in range(3):
        line = Q[n]
        for x in range(16):
            fields[n][4 + x, :, 128:256] = roll(line, 124 - 8 * x, 1)
    line = QE[...]
    for p in range(3):
        EC[20 + p, :, 128:256] = roll(line, 124 - 8 * p, 1)
        EC[1 + p, :, 128:256] = roll(line, 20 - 8 * p, 1)
    for p in range(2):
        ES[20 + p, :, 128:256] = roll(line, 100 - 8 * p, 1)
        ES[2 + p, :, 128:256] = roll(line, 36 - 8 * p, 1)
        EB[20 + p, :, 128:256] = roll(line, 84 - 8 * p, 1)
        EB[2 + p, :, 128:256] = roll(line, 52 - 8 * p, 1)

    def planes(first, last, step, body):
        def some(n, c):
            for j in range(step):
                body(first + n * step + j)
            return c

        lax.fori_loop(0, (last - first) // step, some, 0)

    def valid(i):
        x = ((i >= 4) | (mx > 0)) & ((i < 20) | (mx < NX - 1))
        return YZ[...] * x.astype(jnp.int32) > 0

    def faces(i):
        c = jnp.where(valid(i), EC[i], 0.0)
        EC[i] = c
        FY[i] = 0.5 * (c + roll(c, 23, 0))
        FZ[i] = 0.5 * (c + roll(c, 255, 1))

    planes(0, 24, 4, faces)
    FX[0] = 0.5 * (EC[0] + EC[1])

    def diagonal(i):
        fx = 0.5 * (EC[i] + EC[i + 1])
        FX[i] = fx
        fy, fz = FY[i], FZ[i]
        total = ES[i] + fx + FX[i - 1] + fy + roll(fy, 1, 0) + fz + roll(fz, 1, 1)
        g = jnp.where(valid(i), WEIGHT / total, 0.0)
        G[i] = g
        U0[i] = jnp.where(valid(i), g * EB[i], 0.0)

    planes(1, 23, 2, diagonal)

    def around(i, before, u, after):
        fy, fz = FY[i], FZ[i]
        total = FX[i] * after + FX[i - 1] * before
        total += fy * roll(u, 23, 0) + roll(fy * u, 1, 0)
        return total + (fz * roll(u, 255, 1) + roll(fz * u, 1, 1))

    def first(i):
        v = KEEP * EB[i] + around(i, U0[i - 1], U0[i], U0[i + 1])
        VV[i] = v
        U1[i] = G[i] * v

    def second(i):
        v = KEEP * VV[i] + around(i, U1[i - 1], U1[i], U1[i + 1])
        VV[i] = v
        U2[i] = G[i] * v

    planes(2, 22, 4, first)
    planes(3, 21, 3, second)

    def restrict(n, c):
        total = jnp.zeros((24, 256), F32)
        for j in range(4):
            i = 4 + 4 * n + j
            total += KEEP * VV[i] + around(i, U2[i - 1], U2[i], U2[i + 1])
        total = total[:, 0:128]
        total = total + roll(total, 23, 0)
        total = total + roll(total, 22, 0)
        total = total + roll(total, 127, 1)
        TS[n] = total + roll(total, 126, 1)
        return c

    lax.fori_loop(0, 4, restrict, 0)
    inv_row = INV[0:4]
    inv_lane = 4 * INV[4:8]
    rhs = jnp.zeros((4, 128), F32)
    for r in range(16):
        y = 4 + 4 * (r % 4)
        line = jnp.broadcast_to(TS[r // 4, y : y + 1, :], (4, 128))
        rhs = jnp.where(inv_row == r, jnp.take_along_axis(line, inv_lane, axis=1), rhs)
    inverse = 1.0 / DG[...]
    EBUF[0] = rhs * inverse

    first_half = iota((8, 128), 1) < 64
    row8, lane8 = iota((8, 128), 0), iota((8, 128), 1)
    received = (RB0, RB1, RB2)
    for t, RBUF in enumerate(received):
        for d in COARSE:
            pltpu.make_async_remote_copy(
                src_ref=EBUF.at[t], dst_ref=RBUF.at[slot_of(d)], send_sem=cs.at[t], recv_sem=cr.at[t],
                device_id=device(d), device_id_type=MESH,
            ).start()
        RBUF[0] = EBUF[t]
        arrive(RBUF.at[pl.ds(1, 35)], cr.at[t])

        def fetch(r, c, RBUF=RBUF):
            at = ROWS[r]
            GA[pl.ds(r, 1), :] = RBUF[at >> 2, pl.ds(at & 3, 1), :]
            return c

        lax.fori_loop(0, 32, fetch, 0, unroll=True)
        parts = []
        for k in range(4):
            g = GA[8 * k : 8 * k + 8, :]
            parts.append(jnp.where(PM[8 * k : 8 * k + 8, :] > 0, roll(g, 64, 1), g))
        x = jnp.concatenate(
            [jnp.where(first_half, parts[0], parts[1]), jnp.where(first_half, parts[2], parts[3])], axis=1
        )
        high = x.astype(BF16).astype(F32)
        x = jnp.concatenate([high, x - high], axis=0).astype(BF16)
        y = lax.dot_general(x, W[...], (((1,), (1,)), ((), ())), preferred_element_type=F32)
        y = y[0:8, 0:512] + y[8:16, 0:512] + y[0:8, 512:1024]
        for q in range(4):
            mine = row8 == 2 * q + lane8 // 64
            applied = jnp.sum(jnp.where(mine, y[:, 128 * q : 128 * q + 128], 0.0), axis=0, keepdims=True)
            EBUF[t + 1, q : q + 1, :] = (rhs[q : q + 1] - applied) * inverse[q : q + 1]

    error = EBUF[3]
    err[...] = error
    label = LAB[...]
    field = jnp.zeros((16, 128), F32)
    for q in range(4):
        line = jnp.broadcast_to(error[q : q + 1], (16, 128))
        field = jnp.where(label // 128 == q, jnp.take_along_axis(line, label % 128, axis=1), field)
    for n in range(4):
        FF[n] = field[4 * n : 4 * n + 4]
    for a in (-1, 1, 0):
        for b in (-1, 1, 0):
            for c in (-1, 1, 0):
                if b != 0:
                    send(FF.at[3 * side(b)], RLX.at[side(b), a + 1, c + 1], 10, (a, b, c))
                elif a != 0:
                    send(FF, RLF.at[0 if a < 0 else 1, c + 1], 11, (a, 0, c))
                elif c != 0:
                    send(FF, RLF.at[2, side(c)], 12, (0, 0, c))
    arrive(RLX, rsem.at[10])
    arrive(RLF.at[pl.ds(0, 2)], rsem.at[11])
    arrive(RLF.at[2, pl.ds(0, 2)], rsem.at[12])

    low1 = lane1 < 64
    for n in range(6):
        shown = jnp.int32(1)
        if n == 0:
            shown = (mx > 0).astype(jnp.int32)
        if n == 5:
            shown = (mx < NX - 1).astype(jnp.int32)

        def piece(a, c, yb):
            if n in (0, 5):
                return RLX[0 if n == 5 else 1, a + 1, c + 1, yb : yb + 1]
            if a != 0:
                return RLF[0 if a < 0 else 1, c + 1, n - 1, yb : yb + 1]
            if c != 0:
                return RLF[2, side(c), n - 1, yb : yb + 1]
            return FF[n - 1, yb : yb + 1]

        main, halo = [], []
        for yb in range(-1, 5):
            c, y = (1, 3) if yb < 0 else (-1, 0) if yb > 3 else (0, yb)
            main.append(jnp.broadcast_to(piece(0, c, y), (4, 128)))
            halo.append(jnp.broadcast_to(jnp.where(low1, piece(-1, c, y), piece(1, c, y)), (4, 128)))
        plane = jnp.concatenate([jnp.concatenate(main, axis=0), jnp.concatenate(halo, axis=0)], axis=1)
        LP[n] = jnp.where(YZ[...] * shown > 0, plane, 0.0)

    def corrected(i):
        u = LP[i // 4]
        U2[i] = U0[i] + U1[i] + KEEP * u + G[i] * around(i, LP[(i - 1) // 4], u, LP[(i + 1) // 4])

    def post(i):
        u = U2[i]
        VV[i] = KEEP * u + U0[i] + G[i] * around(i, U2[i - 1], u, U2[i + 1])

    def last(i):
        u = VV[i]
        done = KEEP * u + U0[i] + G[i] * around(i, VV[i - 1], u, VV[i + 1])
        out[i - 4] = done[4:20, 0:128]

    planes(2, 22, 4, corrected)
    planes(3, 21, 3, post)
    planes(4, 20, 4, last)

    for n, buffer in enumerate(arrived):
        arrive(buffer, ssem.at[n])
    for t, RBUF in enumerate(received):
        arrive(RBUF.at[pl.ds(1, 35)], cs.at[t])
    arrive(RLX, ssem.at[10])
    arrive(RLF.at[pl.ds(0, 2)], ssem.at[11])
    arrive(RLF.at[2, pl.ds(0, 2)], ssem.at[12])


def local(source, conductance, storage, aggregate_ids, coarse_values, coarse_columns):
    anywhere = pl.BlockSpec(memory_space=pl.ANY)
    vmem = pl.BlockSpec(memory_space=pltpu.VMEM)
    wide = pltpu.VMEM((24, 24, 256), F32)
    scratch = [pltpu.VMEM((16, 16, 128), F32)] * 3
    scratch += [pltpu.VMEM((4, 16, 128), jnp.int32), pltpu.VMEM((8, 64, 256), F32)]
    sizes = [
        (2, 16, 8, 128), (2, 16, 2, 128), (3, 16, 128), (16, 128), (2, 8, 128),
        (2, 4, 16, 128), (2, 3, 16, 128), (2, 3, 16, 128), (2, 16, 8, 128), (2, 16, 2, 128),
        (2, 2, 3, 8, 128), (2, 3, 16, 128), (2, 2, 8, 128), (2, 2, 16, 128), (2, 2, 2, 8, 128),
    ]
    scratch += [pltpu.VMEM(s, F32) for s in sizes]
    scratch += [wide] * 11
    scratch += [pltpu.VMEM((24, 256), jnp.int32), pltpu.VMEM((3, 24, 128), F32), pltpu.VMEM((24, 128), F32)]
    scratch += [
        pltpu.VMEM((16, 128), jnp.int32),
        pltpu.VMEM((1024, 256), BF16),
        pltpu.VMEM((4, 128), F32),
        pltpu.VMEM((8, 128), jnp.int32),
        pltpu.SMEM((32,), jnp.int32),
        pltpu.VMEM((32, 128), jnp.int32),
        pltpu.VMEM((32, 128), F32),
        pltpu.VMEM((4, 4, 128), F32),
        pltpu.VMEM((4, 24, 128), F32),
        pltpu.VMEM((36, 4, 128), F32),
        pltpu.VMEM((36, 4, 128), F32),
        pltpu.VMEM((36, 4, 128), F32),
        pltpu.VMEM((4, 4, 128), F32),
        pltpu.VMEM((3, 3, 4, 4, 128), F32),
        pltpu.VMEM((2, 3, 3, 4, 128), F32),
        pltpu.VMEM((6, 24, 256), F32),
    ]
    scratch += [pltpu.SemaphoreType.DMA((n,)) for n in (8, 13, 13, 3, 3)]
    solution, error = pl.pallas_call(
        kernel,
        out_shape=(jax.ShapeDtypeStruct((16, 16, 128), F32), jax.ShapeDtypeStruct((4, 128), F32)),
        in_specs=[anywhere] * 5 + [pl.BlockSpec(memory_space=pltpu.SMEM)],
        out_specs=(vmem, vmem),
        scratch_shapes=scratch,
        compiler_params=pltpu.CompilerParams(
            collective_id=0, has_side_effects=True, vmem_limit_bytes=40 * 2**20
        ),
    )(source, conductance, storage, aggregate_ids, coarse_values, coarse_columns)
    return solution, error.reshape(512)


def solution(mesh):
    fine = P("gx", "gy", "grp")
    coarse = ("grp", "gx", "gy")
    return jax.shard_map(
        local,
        mesh=mesh,
        in_specs=(fine, fine, fine, fine, P(coarse, None, None), P(coarse, None)),
        out_specs=(fine, P(coarse)),
        check_vma=False,
    )
```

```python
import functools

import jax
import jax.numpy as jnp
from jax import lax
from jax.sharding import PartitionSpec as P
import jax.experimental.pallas as pl
import jax.experimental.pallas.tpu as pltpu


F32 = jnp.float32
BF16 = jnp.bfloat16
WEIGHT = 2.0 / 3.0
KEEP = 1.0 / 3.0
NG, NX, NY = 4, 16, 8
MESH = pl.DeviceIdType.MESH
STEPS = (-1, 1)

GROUPS = [(-1, -1), (-1, 1), (1, -1), (1, 1), (0, -1), (0, 1), (-1, 0), (1, 0), (0, 0)]


def group_of(x, y):
    return (x % 3) * 3 + y % 3


def members(x, y):
    return [g for g in (2, 1, 3, 0) if (g, x, y) != (0, 0, 0)]


def exists(d):
    place = (lax.axis_index("grp"), lax.axis_index("gx"), lax.axis_index("gy"))
    found = None
    for at, step, count in zip(place, d, (NG, NX, NY)):
        if step:
            here = at > 0 if step < 0 else at < count - 1
            found = here if found is None else found & here
    return found


def when(condition, body):
    if condition is None:
        body()
    else:
        pl.when(condition)(body)


def device(d):
    g, x, y = lax.axis_index("grp"), lax.axis_index("gx"), lax.axis_index("gy")
    return (lax.rem(g + d[0] + NG, NG), lax.rem(x + d[1] + NX, NX), lax.rem(y + d[2] + NY, NY))


def side(step):
    return 0 if step < 0 else 1


def iota(shape, dim):
    return lax.broadcasted_iota(jnp.int32, shape, dim)


def roll(x, shift, axis):
    return pltpu.roll(x, shift, axis)


def arrive(buffer, sem):
    pltpu.make_async_copy(buffer, buffer, sem).wait()


def kernel(
    src, cond, stor, aggr, cval, columns,
    out, err,
    vC, vS, vB, vA, vV, ccol,
    PY8, PY2, PP, PE, PF,
    RXC, RXS, RXB, RY8, RY2, RXY, RP, RF, RE, RK,
    EC, ES, EB, FX, FY, FZ, G, U0, U1, U2, VV, YZ, Q, QE,
    LAB, W, DG, INV, ROWS, PM, GA, EBUF, TS, RB0, RB1, RB2, FF, RLF, RLX, LP,
    lsem, ssem, rsem, cs, cr,
):
    mg, mx, my = lax.axis_index("grp"), lax.axis_index("gx"), lax.axis_index("gy")

    def exchange(messages, base):
        by_direction = {}
        for n, (source, target, d) in enumerate(messages):
            by_direction.setdefault(d, []).append((source, target, base + n))

        def start(d, items):
            for source, target, n in items:
                pltpu.make_async_remote_copy(
                    src_ref=source, dst_ref=target, send_sem=ssem.at[n], recv_sem=rsem.at[n],
                    device_id=device(d), device_id_type=MESH,
                ).start()

        def finish(items, sems):
            for _, target, n in items:
                arrive(target, sems.at[n])

        for d, items in by_direction.items():
            when(exists(d), functools.partial(start, d, items))

        def received():
            for d, items in by_direction.items():
                when(exists(tuple(-step for step in d)), functools.partial(finish, items, rsem))

        def sent():
            for d, items in by_direction.items():
                when(exists(d), functools.partial(finish, items, ssem))

        return received, sent

    loads = [(cond, vC), (stor, vS), (src, vB), (columns, ccol), (cval, vV)]
    loads = [pltpu.make_async_copy(a, b, lsem.at[n]) for n, (a, b) in enumerate(loads)]
    for n in range(4):
        loads.append(pltpu.make_async_copy(aggr.at[4 * n], vA.at[n], lsem.at[5 + n]))
    for copy in loads:
        copy.start()
    barrier = pltpu.get_barrier_semaphore()

    def greet(x, y):
        for g in members(x, y):
            pl.semaphore_signal(barrier, inc=1, device_id=device((g, x, y)), device_id_type=MESH)

    for x, y in GROUPS:
        when(exists((0, x, y)), functools.partial(greet, x, y))
    across = 1 + (mx > 0).astype(jnp.int32) + (mx < NX - 1).astype(jnp.int32)
    along = 1 + (my > 0).astype(jnp.int32) + (my < NY - 1).astype(jnp.int32)
    for copy in loads[:3]:
        copy.wait()

    PY8[0, :, 0:3, :] = vC[:, 0:3, :]
    PY8[0, :, 3:5, :] = vS[:, 0:2, :]
    PY8[0, :, 5:7, :] = vB[:, 0:2, :]
    PY8[0, :, 7:8, :] = vS[:, 2:3, :]
    PY2[0, :, 0:1, :] = vC[:, 3:4, :]
    PY2[0, :, 1:2, :] = vB[:, 2:3, :]
    PY8[1, :, 0:3, :] = vC[:, 13:16, :]
    PY8[1, :, 3:5, :] = vS[:, 14:16, :]
    PY8[1, :, 5:7, :] = vB[:, 14:16, :]
    PY8[1, :, 7:8, :] = vS[:, 13:14, :]
    PY2[1, :, 0:1, :] = vC[:, 12:13, :]
    PY2[1, :, 1:2, :] = vB[:, 13:14, :]
    lane16 = iota((16, 128), 1)
    packed = [jnp.zeros((16, 128), F32)] * 3
    for x in range(16):
        mine = lane16 // 8 == x
        packed = [jnp.where(mine, roll(v[x], 8 * x + 4, 1), p) for v, p in zip((vC, vS, vB), packed)]
    pc, ps, pb = packed
    PP[0], PP[1], PP[2] = pc, ps, pb
    edge = jnp.where(lane16 < 40, roll(ps, 24, 1), roll(pb, 40, 1))
    edge = jnp.where(lane16 >= 64, roll(pb, 88, 1), edge)
    edge = jnp.where(lane16 >= 88, roll(ps, 104, 1), edge)
    PE[...] = jnp.where((lane16 < 24) | (lane16 >= 104), pc, edge)
    PF[0, 0:3], PF[0, 3:5], PF[0, 5:7] = pc[0:3], ps[0:2], pb[0:2]
    PF[1, 0:3], PF[1, 3:5], PF[1, 5:7] = pc[13:16], ps[14:16], pb[14:16]
    PF[0, 7:8] = pc[0:1]
    PF[1, 7:8] = pc[0:1]

    pl.semaphore_wait(barrier, 4 * across * along - 1)
    messages = []
    for b in STEPS:
        messages.append((PY8.at[side(b)], RY8.at[side(b)], (0, 0, b)))
        messages.append((PY2.at[side(b)], RY2.at[side(b)], (0, 0, b)))
    for a in STEPS:
        for b in STEPS:
            for c in STEPS:
                target = RK.at[side(a), side(b), side(c)]
                messages.append((PE.at[pl.ds(8 * side(c), 8)], target, (a, b, c)))
    for b in STEPS:
        s = side(b)
        messages.append((cond.at[pl.ds(12 * s, 4)], RXC.at[s], (0, b, 0)))
        messages.append((stor.at[pl.ds(13 * s, 3)], RXS.at[s], (0, b, 0)))
        messages.append((src.at[pl.ds(13 * s, 3)], RXB.at[s], (0, b, 0)))
    for a in STEPS:
        for b in STEPS:
            messages.append((PE, RE.at[side(a), side(b)], (a, b, 0)))
            messages.append((PF.at[side(b)], RF.at[side(a), side(b)], (a, 0, b)))
            messages.append((PY8.at[side(b), pl.ds(13 * side(a), 3)], RXY.at[side(a), side(b)], (0, a, b)))
    for a in STEPS:
        messages.append((PP, RP.at[side(a)], (a, 0, 0)))
    fine_messages = len(messages)
    halo_received, halo_sent = exchange(messages, 0)

    EC[4:20, 4:20, 0:128] = vC[...]
    ES[4:20, 4:20, 0:128] = vS[...]
    EB[4:20, 4:20, 0:128] = vB[...]
    row, lane = iota((24, 256), 0), iota((24, 256), 1)
    inside = ((row >= 4) | (my > 0)) & ((row < 20) | (my < NY - 1))
    inside &= (lane < 128) | ((lane < 132) & (mg < NG - 1)) | ((lane >= 252) & (mg > 0))
    YZ[...] = inside.astype(jnp.int32)
    for copy in loads[3:]:
        copy.wait()
    for r in range(16):
        LAB[r : r + 1, :] = vA[r // 4, 4 * (r % 4) : 4 * (r % 4) + 1, :]

    def invert(r, inv):
        label = LAB[pl.ds(r, 1), :]
        s8, l8 = iota((8, 128), 0), iota((8, 128), 1)
        mine = (label // 128 == s8 % 4) & (l8 % 4 == 0)
        code = jnp.where(mine, jnp.where(s8 < 4, r, l8 // 4), 0).astype(F32).astype(BF16)
        hot = jnp.where(label % 128 == iota((128, 128), 0), 1.0, 0.0).astype(BF16)
        return inv + lax.dot_general(code, hot, (((1,), (1,)), ((), ())), preferred_element_type=F32)

    inv = lax.fori_loop(0, 16, invert, jnp.zeros((8, 128), F32))
    INV[...] = (inv + 0.5).astype(jnp.int32)

    diag_at = iota((64, 128), 0) == iota((64, 128), 1)
    off_at = iota((64, 256), 0) == iota((64, 256), 1)
    lane1 = iota((1, 128), 1)
    for q in range(4):
        two = []
        for b in (2 * q, 2 * q + 1):
            two.append(jnp.sum(jnp.where(diag_at, vV[b, :, 0:128], 0.0), axis=0, keepdims=True))
            block = jnp.where(off_at, 0.0, vV[b])
            high = block.astype(BF16)
            W[64 * b : 64 * b + 64, :] = high
            W[512 + 64 * b : 576 + 64 * b, :] = (block - high.astype(F32)).astype(BF16)
        DG[q : q + 1, :] = jnp.where(lane1 < 64, two[0], roll(two[1], 64, 1))

    def place(r, c):
        k, b = r // 8, r % 8
        column = ccol[k, b]
        owner, block = column >> 3, column & 7
        dg = (mg - (owner >> 7)) & 3
        dx = lax.rem(mx - ((owner >> 3) & 15) + 3, 3)
        dy = lax.rem(my - (owner & 7) + 3, 3)
        ROWS[r] = ((dx * 3 + dy) * 4 + dg) * 4 + (block >> 1)
        PM[pl.ds(r, 1), :] = jnp.full((1, 128), (block + k) & 1, jnp.int32)
        return c

    lax.fori_loop(0, 32, place, 0)

    halo_received()
    fields = (EC, ES, EB)
    EC[20:24, 4:20, 0:128], EC[0:4, 4:20, 0:128] = RXC[0], RXC[1]
    ES[20:23, 4:20, 0:128], ES[1:4, 4:20, 0:128] = RXS[0], RXS[1]
    EB[20:23, 4:20, 0:128], EB[1:4, 4:20, 0:128] = RXB[0], RXB[1]
    EC[4:20, 20:23, 0:128], EC[4:20, 1:4, 0:128] = RY8[0, :, 0:3], RY8[1, :, 0:3]
    EC[4:20, 23:24, 0:128], EC[4:20, 0:1, 0:128] = RY2[0, :, 0:1], RY2[1, :, 0:1]
    ES[4:20, 20:22, 0:128], ES[4:20, 2:4, 0:128] = RY8[0, :, 3:5], RY8[1, :, 3:5]
    ES[4:20, 22:23, 0:128], ES[4:20, 1:2, 0:128] = RY8[0, :, 7:8], RY8[1, :, 7:8]
    EB[4:20, 20:22, 0:128], EB[4:20, 2:4, 0:128] = RY8[0, :, 5:7], RY8[1, :, 5:7]
    EB[4:20, 22:23, 0:128], EB[4:20, 1:2, 0:128] = RY2[0, :, 1:2], RY2[1, :, 1:2]
    for a in (0, 1):
        x0 = 20 - 19 * a
        EC[x0 : x0 + 3, 20:23, 0:128], EC[x0 : x0 + 3, 1:4, 0:128] = RXY[a, 0, :, 0:3], RXY[a, 1, :, 0:3]
        ES[x0 : x0 + 3, 20:22, 0:128], ES[x0 : x0 + 3, 2:4, 0:128] = RXY[a, 0, :, 3:5], RXY[a, 1, :, 3:5]
        EB[x0 : x0 + 3, 20:22, 0:128], EB[x0 : x0 + 3, 2:4, 0:128] = RXY[a, 0, :, 5:7], RXY[a, 1, :, 5:7]
    low = lane16 % 8 < 4
    low8 = low[0:8]
    for n in range(3):
        Q[n, 4:20] = jnp.where(low, RP[1, n], RP[0, n])
    for b in (0, 1):
        rows = jnp.where(low8, RF[1, b], RF[0, b])
        Q[0, (20, 1)[b] : (23, 4)[b]] = rows[0:3]
        Q[1, (20, 2)[b] : (22, 4)[b]] = rows[3:5]
        Q[2, (20, 2)[b] : (22, 4)[b]] = rows[5:7]
    half, half8 = lane16 < 64, lane16[0:8] < 64
    QE[4:20] = jnp.where(low, jnp.where(half, RE[1, 0], RE[1, 1]), jnp.where(half, RE[0, 0], RE[0, 1]))
    for c in (0, 1):
        rows = jnp.where(
            low8, jnp.where(half8, RK[1, 0, c], RK[1, 1, c]), jnp.where(half8, RK[0, 0, c], RK[0, 1, c])
        )
        QE[(20, 1)[c] : (23, 4)[c]] = rows[(0, 5)[c] : (3, 8)[c]]
    for n in range(3):
        line = Q[n]
        for x in range(16):
            fields[n][4 + x, :, 128:256] = roll(line, 124 - 8 * x, 1)
    line = QE[...]
    for p in range(3):
        EC[20 + p, :, 128:256] = roll(line, 124 - 8 * p, 1)
        EC[1 + p, :, 128:256] = roll(line, 20 - 8 * p, 1)
    for p in range(2):
        ES[20 + p, :, 128:256] = roll(line, 100 - 8 * p, 1)
        ES[2 + p, :, 128:256] = roll(line, 36 - 8 * p, 1)
        EB[20 + p, :, 128:256] = roll(line, 84 - 8 * p, 1)
        EB[2 + p, :, 128:256] = roll(line, 52 - 8 * p, 1)

    def planes(first, last, step, body):
        def some(n, c):
            for j in range(step):
                body(first + n * step + j)
            return c

        lax.fori_loop(0, (last - first) // step, some, 0)

    def valid(i):
        x = ((i >= 4) | (mx > 0)) & ((i < 20) | (mx < NX - 1))
        return YZ[...] * x.astype(jnp.int32) > 0

    def faces(i):
        c = jnp.where(valid(i), EC[i], 0.0)
        EC[i] = c
        EB[i] = jnp.where(valid(i), EB[i], 0.0)
        FY[i] = 0.5 * (c + roll(c, 23, 0))
        FZ[i] = 0.5 * (c + roll(c, 255, 1))

    planes(0, 24, 4, faces)
    FX[0] = 0.5 * (EC[0] + EC[1])

    def diagonal(i):
        fx = 0.5 * (EC[i] + EC[i + 1])
        FX[i] = fx
        fy, fz = FY[i], FZ[i]
        total = ES[i] + fx + FX[i - 1] + fy + roll(fy, 1, 0) + fz + roll(fz, 1, 1)
        g = jnp.where(valid(i), WEIGHT / total, 0.0)
        G[i] = g
        U0[i] = g * EB[i]

    planes(1, 23, 2, diagonal)

    def around(i, before, u, after):
        fy, fz = FY[i], FZ[i]
        total = FX[i] * after + FX[i - 1] * before
        total += fy * roll(u, 23, 0) + roll(fy * u, 1, 0)
        return total + (fz * roll(u, 255, 1) + roll(fz * u, 1, 1))

    def first(i):
        v = KEEP * EB[i] + around(i, U0[i - 1], U0[i], U0[i + 1])
        VV[i] = v
        U1[i] = G[i] * v

    def second(i):
        v = KEEP * VV[i] + around(i, U1[i - 1], U1[i], U1[i + 1])
        VV[i] = v
        U2[i] = G[i] * v

    planes(2, 22, 4, first)
    planes(3, 21, 3, second)

    def restrict(n, c):
        total = jnp.zeros((24, 256), F32)
        for j in range(4):
            i = 4 + 4 * n + j
            total += KEEP * VV[i] + around(i, U2[i - 1], U2[i], U2[i + 1])
        total = total[:, 0:128]
        total = total + roll(total, 23, 0)
        total = total + roll(total, 22, 0)
        total = total + roll(total, 127, 1)
        TS[n] = total + roll(total, 126, 1)
        return c

    lax.fori_loop(0, 4, restrict, 0)
    inv_row = INV[0:4]
    inv_lane = 4 * INV[4:8]
    rhs = jnp.zeros((4, 128), F32)
    for r in range(16):
        y = 4 + 4 * (r % 4)
        line = jnp.broadcast_to(TS[r // 4, y : y + 1, :], (4, 128))
        rhs = jnp.where(inv_row == r, jnp.take_along_axis(line, inv_lane, axis=1), rhs)
    inverse = 1.0 / DG[...]
    EBUF[0] = rhs * inverse

    first_half = iota((8, 128), 1) < 64
    row8, lane8 = iota((8, 128), 0), iota((8, 128), 1)
    received = (RB0, RB1, RB2)
    departures = []
    for t, RBUF in enumerate(received):
        def post_group(x, y, RBUF=RBUF, t=t):
            k = group_of(x, y)
            for g in members(x, y):
                pltpu.make_async_remote_copy(
                    src_ref=EBUF.at[t], dst_ref=RBUF.at[4 * k + g], send_sem=cs.at[t, k], recv_sem=cr.at[t, k],
                    device_id=device((g, x, y)), device_id_type=MESH,
                ).start()

        def end_group(x, y, sems, RBUF=RBUF, t=t):
            k, some = group_of(x, y), members(x, y)
            arrive(RBUF.at[pl.ds(4 * k + 4 - len(some), len(some))], sems.at[t, k])

        for x, y in GROUPS:
            when(exists((0, x, y)), functools.partial(post_group, x, y))
        RBUF[0] = EBUF[t]
        for x, y in GROUPS:
            when(exists((0, -x, -y)), functools.partial(end_group, x, y, cr))
        for x, y in GROUPS:
            departures.append((exists((0, x, y)), functools.partial(end_group, x, y, cs)))

        def fetch(r, c, RBUF=RBUF):
            at = ROWS[r]
            GA[pl.ds(r, 1), :] = RBUF[at >> 2, pl.ds(at & 3, 1), :]
            return c

        lax.fori_loop(0, 32, fetch, 0, unroll=True)
        parts = []
        for k in range(4):
            g = GA[8 * k : 8 * k + 8, :]
            parts.append(jnp.where(PM[8 * k : 8 * k + 8, :] > 0, roll(g, 64, 1), g))
        x = jnp.concatenate(
            [jnp.where(first_half, parts[0], parts[1]), jnp.where(first_half, parts[2], parts[3])], axis=1
        )
        high = x.astype(BF16).astype(F32)
        x = jnp.concatenate([high, x - high], axis=0).astype(BF16)
        y = lax.dot_general(x, W[...], (((1,), (1,)), ((), ())), preferred_element_type=F32)
        y = y[0:8, 0:512] + y[8:16, 0:512] + y[0:8, 512:1024]
        for q in range(4):
            mine = row8 == 2 * q + lane8 // 64
            applied = jnp.sum(jnp.where(mine, y[:, 128 * q : 128 * q + 128], 0.0), axis=0, keepdims=True)
            EBUF[t + 1, q : q + 1, :] = (rhs[q : q + 1] - applied) * inverse[q : q + 1]

    error = EBUF[3]
    err[...] = error
    label = LAB[...]
    field = jnp.zeros((16, 128), F32)
    for q in range(4):
        line = jnp.broadcast_to(error[q : q + 1], (16, 128))
        field = jnp.where(label // 128 == q, jnp.take_along_axis(line, label % 128, axis=1), field)
    for n in range(4):
        FF[n] = field[4 * n : 4 * n + 4]
    messages = []
    for b in (-1, 1, 0):
        for a in (-1, 1, 0):
            for c in (-1, 1, 0):
                if b != 0:
                    messages.append((FF.at[3 * side(b)], RLX.at[side(b), a + 1, c + 1], (a, b, c)))
                elif a != 0:
                    messages.append((FF, RLF.at[side(a), c + 1], (a, 0, c)))
                elif c != 0:
                    messages.append((FF, RLF.at[2, side(c)], (0, 0, c)))
    lifted_received, lifted_sent = exchange(messages, fine_messages)
    lifted_received()

    low1 = lane1 < 64
    for n in range(6):
        shown = jnp.int32(1)
        if n == 0:
            shown = (mx > 0).astype(jnp.int32)
        if n == 5:
            shown = (mx < NX - 1).astype(jnp.int32)

        def piece(a, c, yb):
            if n in (0, 5):
                return RLX[0 if n == 5 else 1, a + 1, c + 1, yb : yb + 1]
            if a != 0:
                return RLF[0 if a < 0 else 1, c + 1, n - 1, yb : yb + 1]
            if c != 0:
                return RLF[2, side(c), n - 1, yb : yb + 1]
            return FF[n - 1, yb : yb + 1]

        main, halo = [], []
        for yb in range(-1, 5):
            c, y = (1, 3) if yb < 0 else (-1, 0) if yb > 3 else (0, yb)
            main.append(jnp.broadcast_to(piece(0, c, y), (4, 128)))
            halo.append(jnp.broadcast_to(jnp.where(low1, piece(-1, c, y), piece(1, c, y)), (4, 128)))
        plane = jnp.concatenate([jnp.concatenate(main, axis=0), jnp.concatenate(halo, axis=0)], axis=1)
        LP[n] = jnp.where(YZ[...] * shown > 0, plane, 0.0)

    def corrected(i):
        u = LP[i // 4]
        U2[i] = U0[i] + U1[i] + KEEP * u + G[i] * around(i, LP[(i - 1) // 4], u, LP[(i + 1) // 4])

    def post(i):
        u = U2[i]
        VV[i] = KEEP * u + U0[i] + G[i] * around(i, U2[i - 1], u, U2[i + 1])

    def last(i):
        u = VV[i]
        done = KEEP * u + U0[i] + G[i] * around(i, VV[i - 1], u, VV[i + 1])
        out[i - 4] = done[4:20, 0:128]

    planes(2, 22, 4, corrected)
    planes(3, 21, 3, post)
    planes(4, 20, 4, last)

    halo_sent()
    for condition, wait in departures:
        when(condition, wait)
    lifted_sent()


def local(source, conductance, storage, aggregate_ids, coarse_values, coarse_columns):
    anywhere = pl.BlockSpec(memory_space=pltpu.HBM)
    vmem = pl.BlockSpec(memory_space=pltpu.VMEM)
    wide = pltpu.VMEM((24, 24, 256), F32)
    scratch = [pltpu.VMEM((16, 16, 128), F32)] * 3
    scratch += [pltpu.VMEM((4, 16, 128), jnp.int32), pltpu.VMEM((8, 64, 256), F32), pltpu.SMEM((4, 8), jnp.int32)]
    sizes = [
        (2, 16, 8, 128), (2, 16, 2, 128), (3, 16, 128), (16, 128), (2, 8, 128),
        (2, 4, 16, 128), (2, 3, 16, 128), (2, 3, 16, 128), (2, 16, 8, 128), (2, 16, 2, 128),
        (2, 2, 3, 8, 128), (2, 3, 16, 128), (2, 2, 8, 128), (2, 2, 16, 128), (2, 2, 2, 8, 128),
    ]
    scratch += [pltpu.VMEM(s, F32) for s in sizes]
    scratch += [wide] * 11
    scratch += [pltpu.VMEM((24, 256), jnp.int32), pltpu.VMEM((3, 24, 128), F32), pltpu.VMEM((24, 128), F32)]
    scratch += [
        pltpu.VMEM((16, 128), jnp.int32),
        pltpu.VMEM((1024, 256), BF16),
        pltpu.VMEM((4, 128), F32),
        pltpu.VMEM((8, 128), jnp.int32),
        pltpu.SMEM((32,), jnp.int32),
        pltpu.VMEM((32, 128), jnp.int32),
        pltpu.VMEM((32, 128), F32),
        pltpu.VMEM((4, 4, 128), F32),
        pltpu.VMEM((4, 24, 128), F32),
        pltpu.VMEM((36, 4, 128), F32),
        pltpu.VMEM((36, 4, 128), F32),
        pltpu.VMEM((36, 4, 128), F32),
        pltpu.VMEM((4, 4, 128), F32),
        pltpu.VMEM((3, 3, 4, 4, 128), F32),
        pltpu.VMEM((2, 3, 3, 4, 128), F32),
        pltpu.VMEM((6, 24, 256), F32),
    ]
    scratch += [pltpu.SemaphoreType.DMA(s) for s in ((9,), (60,), (60,), (3, 9), (3, 9))]
    solution, error = pl.pallas_call(
        kernel,
        out_shape=(jax.ShapeDtypeStruct((16, 16, 128), F32), jax.ShapeDtypeStruct((4, 128), F32)),
        in_specs=[anywhere] * 6,
        out_specs=(vmem, vmem),
        scratch_shapes=scratch,
        compiler_params=pltpu.CompilerParams(
            collective_id=0, has_side_effects=True, vmem_limit_bytes=56_400_000
        ),
    )(source, conductance, storage, aggregate_ids, coarse_values, coarse_columns.T)
    return solution, error.reshape(512)


def solution(mesh):
    fine = P("gx", "gy", "grp")
    coarse = ("grp", "gx", "gy")
    return jax.shard_map(
        local,
        mesh=mesh,
        in_specs=(fine, fine, fine, fine, P(coarse, None, None), P(coarse, None)),
        out_specs=(fine, P(coarse)),
        check_vma=False,
    )
```

```python
import functools

import jax
import jax.numpy as jnp
from jax import lax
from jax.sharding import PartitionSpec as P
import jax.experimental.pallas as pl
import jax.experimental.pallas.tpu as pltpu


F32 = jnp.float32
BF16 = jnp.bfloat16
WEIGHT = 2.0 / 3.0
KEEP = 1.0 / 3.0
NG, NX, NY = 4, 16, 8
MESH = pl.DeviceIdType.MESH
STEPS = (-1, 1)

GROUPS = [(-1, -1), (-1, 1), (1, -1), (1, 1), (0, -1), (0, 1), (-1, 0), (1, 0), (0, 0)]


def group_of(x, y):
    return (x % 3) * 3 + y % 3


def members(x, y):
    return [g for g in (2, 1, 3, 0) if (g, x, y) != (0, 0, 0)]


def exists(d):
    place = (lax.axis_index("grp"), lax.axis_index("gx"), lax.axis_index("gy"))
    found = None
    for at, step, count in zip(place, d, (NG, NX, NY)):
        if step:
            here = at > 0 if step < 0 else at < count - 1
            found = here if found is None else found & here
    return found


def when(condition, body):
    if condition is None:
        body()
    else:
        pl.when(condition)(body)


def device(d):
    g, x, y = lax.axis_index("grp"), lax.axis_index("gx"), lax.axis_index("gy")
    return (lax.rem(g + d[0] + NG, NG), lax.rem(x + d[1] + NX, NX), lax.rem(y + d[2] + NY, NY))


def side(step):
    return 0 if step < 0 else 1


def iota(shape, dim):
    return lax.broadcasted_iota(jnp.int32, shape, dim)


def roll(x, shift, axis):
    return pltpu.roll(x, shift, axis)


def arrive(buffer, sem):
    pltpu.make_async_copy(buffer, buffer, sem).wait()


def kernel(
    src, cond, stor, aggr, cval, columns,
    out, err,
    vC, vS, vB, vA, vV, ccol,
    PY8, PY2, PP, PE, PF,
    RXC, RXS, RXB, RY8, RY2, RXY, RP, RF, RE, RK,
    EC, ES, EB, FX, FY, FZ, G, U0, U1, U2, VV, YZ, Q, QE,
    LAB, W, DG, INV, ROWS, PM, GA, EBUF, TS, RB0, RB1, RB2, FF, RLF, RLX, LP,
    lsem, ssem, rsem, cs, cr,
):
    mg, mx, my = lax.axis_index("grp"), lax.axis_index("gx"), lax.axis_index("gy")

    def exchange(messages, base):
        by_direction = {}
        for n, (source, target, d) in enumerate(messages):
            by_direction.setdefault(d, []).append((source, target, base + n))

        def start(d, items):
            for source, target, n in items:
                pltpu.make_async_remote_copy(
                    src_ref=source, dst_ref=target, send_sem=ssem.at[n], recv_sem=rsem.at[n],
                    device_id=device(d), device_id_type=MESH,
                ).start()

        def finish(items, sems):
            for _, target, n in items:
                arrive(target, sems.at[n])

        for d, items in by_direction.items():
            when(exists(d), functools.partial(start, d, items))

        def received():
            for d, items in by_direction.items():
                when(exists(tuple(-step for step in d)), functools.partial(finish, items, rsem))

        def sent():
            for d, items in by_direction.items():
                when(exists(d), functools.partial(finish, items, ssem))

        return received, sent

    loads = [(cond, vC), (stor, vS), (src, vB), (columns, ccol), (cval, vV)]
    loads = [pltpu.make_async_copy(a, b, lsem.at[n]) for n, (a, b) in enumerate(loads)]
    for n in range(4):
        loads.append(pltpu.make_async_copy(aggr.at[4 * n], vA.at[n], lsem.at[5 + n]))
    for copy in loads:
        copy.start()
    barrier = pltpu.get_barrier_semaphore()

    def greet(x, y):
        for g in members(x, y):
            pl.semaphore_signal(barrier, inc=1, device_id=device((g, x, y)), device_id_type=MESH)

    for x, y in GROUPS:
        when(exists((0, x, y)), functools.partial(greet, x, y))
    across = 1 + (mx > 0).astype(jnp.int32) + (mx < NX - 1).astype(jnp.int32)
    along = 1 + (my > 0).astype(jnp.int32) + (my < NY - 1).astype(jnp.int32)
    for copy in loads[:3]:
        copy.wait()

    PY8[0, :, 0:3, :] = vC[:, 0:3, :]
    PY8[0, :, 3:5, :] = vS[:, 0:2, :]
    PY8[0, :, 5:7, :] = vB[:, 0:2, :]
    PY8[0, :, 7:8, :] = vS[:, 2:3, :]
    PY2[0, :, 0:1, :] = vC[:, 3:4, :]
    PY2[0, :, 1:2, :] = vB[:, 2:3, :]
    PY8[1, :, 0:3, :] = vC[:, 13:16, :]
    PY8[1, :, 3:5, :] = vS[:, 14:16, :]
    PY8[1, :, 5:7, :] = vB[:, 14:16, :]
    PY8[1, :, 7:8, :] = vS[:, 13:14, :]
    PY2[1, :, 0:1, :] = vC[:, 12:13, :]
    PY2[1, :, 1:2, :] = vB[:, 13:14, :]
    lane16 = iota((16, 128), 1)
    packed = [jnp.zeros((16, 128), F32)] * 3
    for x in range(16):
        mine = lane16 // 8 == x
        packed = [jnp.where(mine, roll(v[x], 8 * x + 4, 1), p) for v, p in zip((vC, vS, vB), packed)]
    pc, ps, pb = packed
    PP[0], PP[1], PP[2] = pc, ps, pb
    edge = jnp.where(lane16 < 40, roll(ps, 24, 1), roll(pb, 40, 1))
    edge = jnp.where(lane16 >= 64, roll(pb, 88, 1), edge)
    edge = jnp.where(lane16 >= 88, roll(ps, 104, 1), edge)
    PE[...] = jnp.where((lane16 < 24) | (lane16 >= 104), pc, edge)
    PF[0, 0:3], PF[0, 3:5], PF[0, 5:7] = pc[0:3], ps[0:2], pb[0:2]
    PF[1, 0:3], PF[1, 3:5], PF[1, 5:7] = pc[13:16], ps[14:16], pb[14:16]
    PF[0, 7:8] = pc[0:1]
    PF[1, 7:8] = pc[0:1]

    pl.semaphore_wait(barrier, 4 * across * along - 1)
    messages = []
    for b in STEPS:
        messages.append((PY8.at[side(b)], RY8.at[side(b)], (0, 0, b)))
        messages.append((PY2.at[side(b)], RY2.at[side(b)], (0, 0, b)))
    for a in STEPS:
        for b in STEPS:
            for c in STEPS:
                target = RK.at[side(a), side(b), side(c)]
                messages.append((PE.at[pl.ds(8 * side(c), 8)], target, (a, b, c)))
    for b in STEPS:
        s = side(b)
        messages.append((cond.at[pl.ds(12 * s, 4)], RXC.at[s], (0, b, 0)))
        messages.append((stor.at[pl.ds(13 * s, 3)], RXS.at[s], (0, b, 0)))
        messages.append((src.at[pl.ds(13 * s, 3)], RXB.at[s], (0, b, 0)))
    for a in STEPS:
        for b in STEPS:
            messages.append((PE, RE.at[side(a), side(b)], (a, b, 0)))
            messages.append((PF.at[side(b)], RF.at[side(a), side(b)], (a, 0, b)))
            messages.append((PY8.at[side(b), pl.ds(13 * side(a), 3)], RXY.at[side(a), side(b)], (0, a, b)))
    for a in STEPS:
        messages.append((PP, RP.at[side(a)], (a, 0, 0)))
    fine_messages = len(messages)
    halo_received, halo_sent = exchange(messages, 0)

    EC[4:20, 4:20, 0:128] = vC[...]
    ES[4:20, 4:20, 0:128] = vS[...]
    EB[4:20, 4:20, 0:128] = vB[...]
    row, lane = iota((24, 256), 0), iota((24, 256), 1)
    inside = ((row >= 4) | (my > 0)) & ((row < 20) | (my < NY - 1))
    inside &= (lane < 128) | ((lane < 132) & (mg < NG - 1)) | ((lane >= 252) & (mg > 0))
    YZ[...] = inside.astype(jnp.int32)
    for copy in loads[3:]:
        copy.wait()
    for r in range(16):
        LAB[r : r + 1, :] = vA[r // 4, 4 * (r % 4) : 4 * (r % 4) + 1, :]

    def invert(r, inv):
        label = LAB[pl.ds(r, 1), :]
        s8, l8 = iota((8, 128), 0), iota((8, 128), 1)
        mine = (label // 128 == s8 % 4) & (l8 % 4 == 0)
        code = jnp.where(mine, jnp.where(s8 < 4, r, l8 // 4), 0).astype(F32).astype(BF16)
        hot = jnp.where(label % 128 == iota((128, 128), 0), 1.0, 0.0).astype(BF16)
        return inv + lax.dot_general(code, hot, (((1,), (1,)), ((), ())), preferred_element_type=F32)

    inv = lax.fori_loop(0, 16, invert, jnp.zeros((8, 128), F32))
    INV[...] = (inv + 0.5).astype(jnp.int32)

    diag_at = iota((64, 128), 0) == iota((64, 128), 1)
    off_at = iota((64, 256), 0) == iota((64, 256), 1)
    lane1 = iota((1, 128), 1)
    for q in range(4):
        two = []
        for b in (2 * q, 2 * q + 1):
            two.append(jnp.sum(jnp.where(diag_at, vV[b, :, 0:128], 0.0), axis=0, keepdims=True))
            block = jnp.where(off_at, 0.0, vV[b])
            high = block.astype(BF16)
            W[64 * b : 64 * b + 64, :] = high
            W[512 + 64 * b : 576 + 64 * b, :] = (block - high.astype(F32)).astype(BF16)
        DG[q : q + 1, :] = jnp.where(lane1 < 64, two[0], roll(two[1], 64, 1))

    def place(r, c):
        k, b = r // 8, r % 8
        column = ccol[k, b]
        owner, block = column >> 3, column & 7
        dg = (mg - (owner >> 7)) & 3
        dx = lax.rem(mx - ((owner >> 3) & 15) + 3, 3)
        dy = lax.rem(my - (owner & 7) + 3, 3)
        ROWS[r] = ((dx * 3 + dy) * 4 + dg) * 4 + (block >> 1)
        PM[pl.ds(r, 1), :] = jnp.full((1, 128), (block + k) & 1, jnp.int32)
        return c

    lax.fori_loop(0, 32, place, 0)

    halo_received()
    fields = (EC, ES, EB)
    EC[20:24, 4:20, 0:128], EC[0:4, 4:20, 0:128] = RXC[0], RXC[1]
    ES[20:23, 4:20, 0:128], ES[1:4, 4:20, 0:128] = RXS[0], RXS[1]
    EB[20:23, 4:20, 0:128], EB[1:4, 4:20, 0:128] = RXB[0], RXB[1]
    EC[4:20, 20:23, 0:128], EC[4:20, 1:4, 0:128] = RY8[0, :, 0:3], RY8[1, :, 0:3]
    EC[4:20, 23:24, 0:128], EC[4:20, 0:1, 0:128] = RY2[0, :, 0:1], RY2[1, :, 0:1]
    ES[4:20, 20:22, 0:128], ES[4:20, 2:4, 0:128] = RY8[0, :, 3:5], RY8[1, :, 3:5]
    ES[4:20, 22:23, 0:128], ES[4:20, 1:2, 0:128] = RY8[0, :, 7:8], RY8[1, :, 7:8]
    EB[4:20, 20:22, 0:128], EB[4:20, 2:4, 0:128] = RY8[0, :, 5:7], RY8[1, :, 5:7]
    EB[4:20, 22:23, 0:128], EB[4:20, 1:2, 0:128] = RY2[0, :, 1:2], RY2[1, :, 1:2]
    for a in (0, 1):
        x0 = 20 - 19 * a
        EC[x0 : x0 + 3, 20:23, 0:128], EC[x0 : x0 + 3, 1:4, 0:128] = RXY[a, 0, :, 0:3], RXY[a, 1, :, 0:3]
        ES[x0 : x0 + 3, 20:22, 0:128], ES[x0 : x0 + 3, 2:4, 0:128] = RXY[a, 0, :, 3:5], RXY[a, 1, :, 3:5]
        EB[x0 : x0 + 3, 20:22, 0:128], EB[x0 : x0 + 3, 2:4, 0:128] = RXY[a, 0, :, 5:7], RXY[a, 1, :, 5:7]
    low = lane16 % 8 < 4
    low8 = low[0:8]
    for n in range(3):
        Q[n, 4:20] = jnp.where(low, RP[1, n], RP[0, n])
    for b in (0, 1):
        rows = jnp.where(low8, RF[1, b], RF[0, b])
        Q[0, (20, 1)[b] : (23, 4)[b]] = rows[0:3]
        Q[1, (20, 2)[b] : (22, 4)[b]] = rows[3:5]
        Q[2, (20, 2)[b] : (22, 4)[b]] = rows[5:7]
    half, half8 = lane16 < 64, lane16[0:8] < 64
    QE[4:20] = jnp.where(low, jnp.where(half, RE[1, 0], RE[1, 1]), jnp.where(half, RE[0, 0], RE[0, 1]))
    for c in (0, 1):
        rows = jnp.where(
            low8, jnp.where(half8, RK[1, 0, c], RK[1, 1, c]), jnp.where(half8, RK[0, 0, c], RK[0, 1, c])
        )
        QE[(20, 1)[c] : (23, 4)[c]] = rows[(0, 5)[c] : (3, 8)[c]]
    for n in range(3):
        line = Q[n]
        for x in range(16):
            fields[n][4 + x, :, 128:256] = roll(line, 124 - 8 * x, 1)
    line = QE[...]
    for p in range(3):
        EC[20 + p, :, 128:256] = roll(line, 124 - 8 * p, 1)
        EC[1 + p, :, 128:256] = roll(line, 20 - 8 * p, 1)
    for p in range(2):
        ES[20 + p, :, 128:256] = roll(line, 100 - 8 * p, 1)
        ES[2 + p, :, 128:256] = roll(line, 36 - 8 * p, 1)
        EB[20 + p, :, 128:256] = roll(line, 84 - 8 * p, 1)
        EB[2 + p, :, 128:256] = roll(line, 52 - 8 * p, 1)

    def planes(first, last, step, body):
        def some(n, c):
            for j in range(step):
                body(first + n * step + j)
            return c

        lax.fori_loop(0, (last - first) // step, some, 0, unroll=True)

    def valid(i):
        x = ((i >= 4) | (mx > 0)) & ((i < 20) | (mx < NX - 1))
        return YZ[...] * x.astype(jnp.int32) > 0

    def faces(i):
        c = jnp.where(valid(i), EC[i], 0.0)
        EC[i] = c
        EB[i] = jnp.where(valid(i), EB[i], 0.0)
        FY[i] = 0.5 * (c + roll(c, 23, 0))
        FZ[i] = 0.5 * (c + roll(c, 255, 1))

    planes(0, 24, 4, faces)
    FX[0] = 0.5 * (EC[0] + EC[1])

    def diagonal(i):
        fx = 0.5 * (EC[i] + EC[i + 1])
        FX[i] = fx
        fy, fz = FY[i], FZ[i]
        total = ES[i] + fx + FX[i - 1] + fy + roll(fy, 1, 0) + fz + roll(fz, 1, 1)
        g = jnp.where(valid(i), WEIGHT / total, 0.0)
        G[i] = g
        U0[i] = g * EB[i]

    planes(1, 23, 2, diagonal)

    def around(i, before, u, after):
        fy, fz = FY[i], FZ[i]
        total = FX[i] * after + FX[i - 1] * before
        total += fy * roll(u, 23, 0) + roll(fy * u, 1, 0)
        return total + (fz * roll(u, 255, 1) + roll(fz * u, 1, 1))

    def first(i):
        v = KEEP * EB[i] + around(i, U0[i - 1], U0[i], U0[i + 1])
        VV[i] = v
        U1[i] = G[i] * v

    def second(i):
        v = KEEP * VV[i] + around(i, U1[i - 1], U1[i], U1[i + 1])
        VV[i] = v
        U2[i] = G[i] * v

    planes(2, 22, 4, first)
    planes(3, 21, 3, second)

    def restrict(n, c):
        total = jnp.zeros((24, 256), F32)
        for j in range(4):
            i = 4 + 4 * n + j
            total += KEEP * VV[i] + around(i, U2[i - 1], U2[i], U2[i + 1])
        total = total[:, 0:128]
        total = total + roll(total, 23, 0)
        total = total + roll(total, 22, 0)
        total = total + roll(total, 127, 1)
        TS[n] = total + roll(total, 126, 1)
        return c

    lax.fori_loop(0, 4, restrict, 0, unroll=True)
    inv_row = INV[0:4]
    inv_lane = 4 * INV[4:8]
    rhs = jnp.zeros((4, 128), F32)
    for r in range(16):
        y = 4 + 4 * (r % 4)
        line = jnp.broadcast_to(TS[r // 4, y : y + 1, :], (4, 128))
        rhs = jnp.where(inv_row == r, jnp.take_along_axis(line, inv_lane, axis=1), rhs)
    inverse = 1.0 / DG[...]
    EBUF[0] = rhs * inverse

    first_half = iota((8, 128), 1) < 64
    row8, lane8 = iota((8, 128), 0), iota((8, 128), 1)
    received = (RB0, RB1, RB2)
    departures = []
    for t, RBUF in enumerate(received):
        def post_group(x, y, RBUF=RBUF, t=t):
            k = group_of(x, y)
            for g in members(x, y):
                pltpu.make_async_remote_copy(
                    src_ref=EBUF.at[t], dst_ref=RBUF.at[4 * k + g], send_sem=cs.at[t, k], recv_sem=cr.at[t, k],
                    device_id=device((g, x, y)), device_id_type=MESH,
                ).start()

        def end_group(x, y, sems, RBUF=RBUF, t=t):
            k, some = group_of(x, y), members(x, y)
            arrive(RBUF.at[pl.ds(4 * k + 4 - len(some), len(some))], sems.at[t, k])

        for x, y in GROUPS:
            when(exists((0, x, y)), functools.partial(post_group, x, y))
        RBUF[0] = EBUF[t]
        for x, y in GROUPS:
            when(exists((0, -x, -y)), functools.partial(end_group, x, y, cr))
        for x, y in GROUPS:
            departures.append((exists((0, x, y)), functools.partial(end_group, x, y, cs)))

        def fetch(r, c, RBUF=RBUF):
            at = ROWS[r]
            GA[pl.ds(r, 1), :] = RBUF[at >> 2, pl.ds(at & 3, 1), :]
            return c

        lax.fori_loop(0, 32, fetch, 0, unroll=True)
        parts = []
        for k in range(4):
            g = GA[8 * k : 8 * k + 8, :]
            parts.append(jnp.where(PM[8 * k : 8 * k + 8, :] > 0, roll(g, 64, 1), g))
        x = jnp.concatenate(
            [jnp.where(first_half, parts[0], parts[1]), jnp.where(first_half, parts[2], parts[3])], axis=1
        )
        high = x.astype(BF16).astype(F32)
        x = jnp.concatenate([high, x - high], axis=0).astype(BF16)
        y = lax.dot_general(x, W[...], (((1,), (1,)), ((), ())), preferred_element_type=F32)
        y = y[0:8, 0:512] + y[8:16, 0:512] + y[0:8, 512:1024]
        for q in range(4):
            mine = row8 == 2 * q + lane8 // 64
            applied = jnp.sum(jnp.where(mine, y[:, 128 * q : 128 * q + 128], 0.0), axis=0, keepdims=True)
            EBUF[t + 1, q : q + 1, :] = (rhs[q : q + 1] - applied) * inverse[q : q + 1]

    error = EBUF[3]
    err[...] = error
    label = LAB[...]
    field = jnp.zeros((16, 128), F32)
    for q in range(4):
        line = jnp.broadcast_to(error[q : q + 1], (16, 128))
        field = jnp.where(label // 128 == q, jnp.take_along_axis(line, label % 128, axis=1), field)
    for n in range(4):
        FF[n] = field[4 * n : 4 * n + 4]
    messages = []
    for b in (-1, 1, 0):
        for a in (-1, 1, 0):
            for c in (-1, 1, 0):
                if b != 0:
                    messages.append((FF.at[3 * side(b)], RLX.at[side(b), a + 1, c + 1], (a, b, c)))
                elif a != 0:
                    messages.append((FF, RLF.at[side(a), c + 1], (a, 0, c)))
                elif c != 0:
                    messages.append((FF, RLF.at[2, side(c)], (0, 0, c)))
    lifted_received, lifted_sent = exchange(messages, fine_messages)
    lifted_received()

    low1 = lane1 < 64
    for n in range(6):
        shown = jnp.int32(1)
        if n == 0:
            shown = (mx > 0).astype(jnp.int32)
        if n == 5:
            shown = (mx < NX - 1).astype(jnp.int32)

        def piece(a, c, yb):
            if n in (0, 5):
                return RLX[0 if n == 5 else 1, a + 1, c + 1, yb : yb + 1]
            if a != 0:
                return RLF[0 if a < 0 else 1, c + 1, n - 1, yb : yb + 1]
            if c != 0:
                return RLF[2, side(c), n - 1, yb : yb + 1]
            return FF[n - 1, yb : yb + 1]

        main, halo = [], []
        for yb in range(-1, 5):
            c, y = (1, 3) if yb < 0 else (-1, 0) if yb > 3 else (0, yb)
            main.append(jnp.broadcast_to(piece(0, c, y), (4, 128)))
            halo.append(jnp.broadcast_to(jnp.where(low1, piece(-1, c, y), piece(1, c, y)), (4, 128)))
        plane = jnp.concatenate([jnp.concatenate(main, axis=0), jnp.concatenate(halo, axis=0)], axis=1)
        LP[n] = jnp.where(YZ[...] * shown > 0, plane, 0.0)

    def corrected(i):
        u = LP[i // 4]
        U2[i] = U0[i] + U1[i] + KEEP * u + G[i] * around(i, LP[(i - 1) // 4], u, LP[(i + 1) // 4])

    def post(i):
        u = U2[i]
        VV[i] = KEEP * u + U0[i] + G[i] * around(i, U2[i - 1], u, U2[i + 1])

    def last(i):
        u = VV[i]
        done = KEEP * u + U0[i] + G[i] * around(i, VV[i - 1], u, VV[i + 1])
        out[i - 4] = done[4:20, 0:128]

    planes(2, 22, 4, corrected)
    planes(3, 21, 3, post)
    planes(4, 20, 4, last)

    halo_sent()
    for condition, wait in departures:
        when(condition, wait)
    lifted_sent()


def local(source, conductance, storage, aggregate_ids, coarse_values, coarse_columns):
    anywhere = pl.BlockSpec(memory_space=pltpu.HBM)
    vmem = pl.BlockSpec(memory_space=pltpu.VMEM)
    wide = pltpu.VMEM((24, 24, 256), F32)
    scratch = [pltpu.VMEM((16, 16, 128), F32)] * 3
    scratch += [pltpu.VMEM((4, 16, 128), jnp.int32), pltpu.VMEM((8, 64, 256), F32), pltpu.SMEM((4, 8), jnp.int32)]
    sizes = [
        (2, 16, 8, 128), (2, 16, 2, 128), (3, 16, 128), (16, 128), (2, 8, 128),
        (2, 4, 16, 128), (2, 3, 16, 128), (2, 3, 16, 128), (2, 16, 8, 128), (2, 16, 2, 128),
        (2, 2, 3, 8, 128), (2, 3, 16, 128), (2, 2, 8, 128), (2, 2, 16, 128), (2, 2, 2, 8, 128),
    ]
    scratch += [pltpu.VMEM(s, F32) for s in sizes]
    scratch += [wide] * 11
    scratch += [pltpu.VMEM((24, 256), jnp.int32), pltpu.VMEM((3, 24, 128), F32), pltpu.VMEM((24, 128), F32)]
    scratch += [
        pltpu.VMEM((16, 128), jnp.int32),
        pltpu.VMEM((1024, 256), BF16),
        pltpu.VMEM((4, 128), F32),
        pltpu.VMEM((8, 128), jnp.int32),
        pltpu.SMEM((32,), jnp.int32),
        pltpu.VMEM((32, 128), jnp.int32),
        pltpu.VMEM((32, 128), F32),
        pltpu.VMEM((4, 4, 128), F32),
        pltpu.VMEM((4, 24, 128), F32),
        pltpu.VMEM((36, 4, 128), F32),
        pltpu.VMEM((36, 4, 128), F32),
        pltpu.VMEM((36, 4, 128), F32),
        pltpu.VMEM((4, 4, 128), F32),
        pltpu.VMEM((3, 3, 4, 4, 128), F32),
        pltpu.VMEM((2, 3, 3, 4, 128), F32),
        pltpu.VMEM((6, 24, 256), F32),
    ]
    scratch += [pltpu.SemaphoreType.DMA(s) for s in ((9,), (60,), (60,), (3, 9), (3, 9))]
    solution, error = pl.pallas_call(
        kernel,
        out_shape=(jax.ShapeDtypeStruct((16, 16, 128), F32), jax.ShapeDtypeStruct((4, 128), F32)),
        in_specs=[anywhere] * 6,
        out_specs=(vmem, vmem),
        scratch_shapes=scratch,
        compiler_params=pltpu.CompilerParams(
            collective_id=0, has_side_effects=True, vmem_limit_bytes=56_400_000
        ),
    )(source, conductance, storage, aggregate_ids, coarse_values, coarse_columns.T)
    return solution, error.reshape(512)


def solution(mesh):
    fine = P("gx", "gy", "grp")
    coarse = ("grp", "gx", "gy")
    return jax.shard_map(
        local,
        mesh=mesh,
        in_specs=(fine, fine, fine, fine, P(coarse, None, None), P(coarse, None)),
        out_specs=(fine, P(coarse)),
        check_vma=False,
    )
```
